32 devices in a mesh: dp: 4 (over y, x), seq: 8 (over z, core).
Axes of the slice: x: 2, y: 2, z: 4, core: 2. Of those that a mesh axis runs over, the one named last changes fastest.
Arguments:
- tokens: bfloat16 [4, 1024, 5120], P('dp', 'seq'), may hold values from -6 to 6
- base_query: bfloat16 [4, 1024, 2560], P('dp', 'seq'), may hold values from -96 to 96
- k_base: bfloat16 [4, 1024, 2560], P('dp', 'seq'), may hold values from -4 to 4
- v_base: bfloat16 [4, 1024, 2560], P('dp', 'seq'), may hold values from -6 to 6
- cotangent: bfloat16 [4, 1024, 2560], P('dp', 'seq'), may hold values from -0.018676758 to 0.018676758
- adapter_down: bfloat16 [5120, 256], replicated, may hold values from -0.078125 to 0.078125
- adapter_up_weight: bfloat16 [256, 2560], replicated, may hold values from -1 to 1
- gate_weight: bfloat16 [8, 5120], replicated, may hold values from -0.078125 to 0.078125
Outputs:
- attended: bfloat16 [4, 1024, 2560], P('dp', 'seq')
- gate_grad: float32 [8, 5120], replicated
The draws below stay inside these ranges and needn't reach their ends.
All inputs are finite; a program needn't handle non-finite values.
Results may differ from the reference program's by a relative error of at most 0.03.
Values may be sent and summed in bfloat16 or wider, within the bound.
A program may use at most 192 MiB of HBM per device.

```python
import jax
import jax.numpy as jnp
from jax import lax

D = 5120
HEAD_DIM = 128
HEADS = 20
EXPERTS = 8
RANK = 32
TOK_DEV = 128
LENGTH = 1024
BATCH = 4
N_DP = 4
N_SEQ = 8


def drawn_pair(key):
    shape = (BATCH, LENGTH, HEADS * HEAD_DIM)
    key_rows = jnp.clip(jax.random.normal(jax.random.fold_in(key, 7), shape, jnp.float32), -4.0, 4.0)
    query_rows = jnp.clip(jax.random.normal(jax.random.fold_in(key, 5), shape, jnp.float32), -4.0, 4.0)
    return (query_rows, key_rows)


def draw_base_query(key, part):
    return drawn_pair(key)[0].astype(jnp.bfloat16)


def draw_k_base(key, part):
    return drawn_pair(key)[1].astype(jnp.bfloat16)


def block_scale(rng, extent, split, low, top_value):
    level = 1.0
    for axis_at, shards_of in split:
        steps = jax.random.uniform(jax.random.fold_in(jax.random.fold_in(rng, 6), axis_at), (shards_of,), jnp.float32, low / len(split), top_value / len(split))
        level = level * jnp.repeat(jnp.exp(steps), extent[axis_at] // shards_of).reshape((-1,) + (1,) * (len(extent) - 1 - axis_at))
    return level


def normal_values(rng, shape, spread, limit, pieces=(), kind=jnp.bfloat16):
    values = spread * jax.random.normal(rng, shape, jnp.float32)
    if pieces:
        values = values * block_scale(rng, shape, pieces, -0.22, 0.18)
    return jnp.clip(values, -limit, limit).astype(kind)


def setup_inputs(seed: int = 0) -> dict:
    keys = jax.random.split(jax.random.key(seed), 9)
    return {
        "tokens": normal_values(keys[0], (BATCH, LENGTH, D), 1.0, 6.0, ((0, 4), (1, 8))),
        "base_query": draw_base_query(jax.random.fold_in(keys[8], 71), 0),
        "k_base": draw_k_base(jax.random.fold_in(keys[8], 71), 0),
        "v_base": normal_values(keys[3], (BATCH, LENGTH, HEADS * HEAD_DIM), 1.0, 6.0, ((0, 4), (1, 8))),
        "cotangent": normal_values(keys[4], (BATCH, LENGTH, HEADS * HEAD_DIM), (0.2 / (TOK_DEV * N_SEQ * N_DP) ** 0.5), 0.018676758, ((0, 4), (1, 8))),
        "adapter_down": normal_values(keys[5], (D, EXPERTS * RANK), D ** -0.5, 0.078125),
        "adapter_up_weight": normal_values(keys[6], (EXPERTS * RANK, HEADS * HEAD_DIM), RANK ** -0.5, 1.0),
        "gate_weight": normal_values(keys[7], (EXPERTS, D), D ** -0.5, 0.078125),
    }


adapter_scale = 2.0
masked_score = -1e30


def reference(tokens, base_query, k_base, v_base, cotangent, adapter_down, adapter_up_weight, gate_weight):
    width = HEADS * HEAD_DIM
    score_scale = HEAD_DIM ** -0.5
    block = min(LENGTH, 256)
    block_count = LENGTH // block

    def per_sequence(inputs):
        seq_tokens, sequence_query, seq_keys, seq_values, seq_cot = inputs
        logits = jnp.dot(seq_tokens, gate_weight.T, preferred_element_type=jnp.float32)
        gates = jax.nn.softmax(logits, axis=-1)
        low = jnp.dot(seq_tokens, adapter_down, preferred_element_type=jnp.float32).astype(jnp.bfloat16)
        blended_query = (low.astype(jnp.float32) * jnp.repeat(gates, RANK, axis=1)).astype(jnp.bfloat16)
        query_matrix = (sequence_query.astype(jnp.float32) + adapter_scale * jnp.dot(blended_query, adapter_up_weight, preferred_element_type=jnp.float32)).astype(jnp.bfloat16)
        query_heads = query_matrix.reshape(LENGTH, HEADS, HEAD_DIM).astype(jnp.float32)
        key_heads = seq_keys.reshape(LENGTH, HEADS, HEAD_DIM).astype(jnp.float32)
        value_heads = seq_values.reshape(LENGTH, HEADS, HEAD_DIM).astype(jnp.float32)
        cot_heads = seq_cot.reshape(LENGTH, HEADS, HEAD_DIM).astype(jnp.float32)
        key_positions = jnp.arange(LENGTH, dtype=jnp.int32)

        def one_block(block_index):
            first_row = (block_index * block).astype(jnp.int32)
            query_rows = lax.dynamic_slice_in_dim(query_heads, first_row, block, 0)
            cot_rows = lax.dynamic_slice_in_dim(cot_heads, first_row, block, 0)
            positions = first_row + jnp.arange(block, dtype=jnp.int32)
            scores = jnp.einsum("qhd,khd->qhk", query_rows, key_heads, precision=lax.Precision.HIGHEST) * score_scale
            visible = key_positions[None, None, :] <= positions[:, None, None]
            scores = jnp.where(visible, scores, masked_score)
            probabilities = jax.nn.softmax(scores, axis=-1)
            probabilities_b = probabilities.astype(jnp.bfloat16).astype(jnp.float32)
            attended_rows = jnp.einsum("qhk,khd->qhd", probabilities_b, value_heads, precision=lax.Precision.HIGHEST)
            slopes = jnp.einsum("qhd,khd->qhk", cot_rows, value_heads, precision=lax.Precision.HIGHEST)
            products = probabilities * slopes
            delta = jnp.sum(products, axis=-1)
            scaled = products.astype(jnp.bfloat16).astype(jnp.float32)
            grad_part = jnp.einsum("qhk,khd->qhd", scaled, key_heads, precision=lax.Precision.HIGHEST)
            key_part = jnp.einsum("qhk,khd->qhd", probabilities_b, key_heads, precision=lax.Precision.HIGHEST)
            dquery_rows = score_scale * (grad_part - delta[..., None] * key_part)
            return attended_rows.astype(jnp.bfloat16), dquery_rows.astype(jnp.bfloat16)

        attended_blocks, dquery_blocks = lax.map(one_block, jnp.arange(block_count, dtype=jnp.int32))
        attended = attended_blocks.reshape(LENGTH, width)
        query_gradient = dquery_blocks.reshape(LENGTH, width)
        blended_query_gradient = adapter_scale * jnp.dot(query_gradient, adapter_up_weight.T, preferred_element_type=jnp.float32)
        dgates = (blended_query_gradient * low.astype(jnp.float32)).reshape(LENGTH, EXPERTS, RANK).sum(axis=-1)
        dlogits = gates * (dgates - jnp.sum(gates * dgates, axis=-1, keepdims=True))
        partial_grad = jnp.dot(dlogits.astype(jnp.bfloat16).T, seq_tokens, preferred_element_type=jnp.float32)
        return attended, partial_grad

    attended_all, partials = lax.map(per_sequence, (tokens, base_query, k_base, v_base, cotangent))
    return attended_all, jnp.sum(partials, axis=0)
```

```python
import functools

import jax
import jax.numpy as jnp
from jax import lax
from jax.experimental import pallas as pl
from jax.experimental.pallas import tpu as pltpu
from jax.sharding import PartitionSpec as P

HEAD_DIM = 128
ADAPTER_SCALE = 2.0
MASKED = -1e30
MESH = pl.DeviceIdType.MESH
F32 = jnp.float32
BF16 = jnp.bfloat16
NT = (((1,), (1,)), ((), ()))
NN = (((1,), (0,)), ((), ()))


def dot(a, b, dims=NN, precision=None):
    return lax.dot_general(a, b, dims, preferred_element_type=F32, precision=precision)


def kernel(
    chips, chunks, heads, n_dp,
    k_hbm, v_hbm, bq_hbm, cot_hbm, tok_hbm, down_hbm, up_hbm, gw_hbm,
    out_ref, gg_ref,
    kv, bq, cot, tok, down, up, gw, low, mixed, dmix, gates_ref, part, ra, rb, rc, mine,
    own_sem, load_sem, up_send, up_recv, mate_send, mate_recv,
    a_send, a_recv, b_send, b_recv, c_send, c_recv,
):
    n_seq = 2 * chips
    me = lax.axis_index("seq")
    dp = lax.axis_index("dp")
    z = me // 2
    core = lax.rem(me, 2)
    mate = me + 1 - 2 * core
    rows = tok.shape[0]
    wide = heads * HEAD_DIM
    scale = HEAD_DIM ** (-0.5)

    barrier = pltpu.get_barrier_semaphore()
    for d in range(1, n_seq):
        pl.semaphore_signal(
            barrier, inc=1, device_id={"seq": lax.rem(me + d, n_seq)}, device_id_type=MESH
        )
    for d in range(1, n_dp):
        pl.semaphore_signal(
            barrier, inc=1, device_id={"dp": lax.rem(dp + d, n_dp)}, device_id_type=MESH
        )

    def own_copies(c):
        cols = pl.ds(c * wide, wide)
        return [
            pltpu.make_async_copy(src.at[0, :, cols], kv.at[c, z, core, i], own_sem.at[c, i])
            for i, src in enumerate((k_hbm, v_hbm))
        ]

    for c in range(chunks):
        for copy in own_copies(c):
            copy.start()
    loads = [
        pltpu.make_async_copy(src, dst, load_sem.at[i])
        for i, (src, dst) in enumerate(
            (
                (tok_hbm.at[0], tok), (gw_hbm, gw), (down_hbm, down), (up_hbm, up),
                (bq_hbm.at[0], bq), (cot_hbm.at[0], cot),
            )
        )
    ]
    for copy in loads:
        copy.start()
    pl.semaphore_wait(barrier, n_seq - 1 + n_dp - 1)

    def to_next(c, j):
        block = kv.at[c, j, core]
        return pltpu.make_async_remote_copy(
            src_ref=block, dst_ref=block, send_sem=up_send.at[c, j], recv_sem=up_recv.at[c, j],
            device_id={"seq": lax.rem(me + 2, n_seq)}, device_id_type=MESH,
        )

    def to_mate(c, j):
        block = kv.at[c, j, core]
        return pltpu.make_async_remote_copy(
            src_ref=block, dst_ref=block, send_sem=mate_send.at[c, j], recv_sem=mate_recv.at[c, j],
            device_id={"seq": mate}, device_id_type=MESH,
        )

    def from_mate(c, j):
        block = kv.at[c, j, 1 - core]
        return pltpu.make_async_remote_copy(
            src_ref=block, dst_ref=block, send_sem=mate_send.at[c, j], recv_sem=mate_recv.at[c, j],
            device_id={"seq": mate}, device_id_type=MESH,
        )

    for c in range(chunks):
        for copy in own_copies(c):
            copy.wait()

        @pl.when(z < chips - 1)
        def _():
            to_next(c, z).start()

        to_mate(c, z).start()

    loads[0].wait()
    loads[1].wait()
    logits = dot(tok[...], gw[...], NT)
    logits = jnp.exp(logits - jnp.max(logits, axis=-1, keepdims=True))
    gates = logits / jnp.sum(logits, axis=-1, keepdims=True)
    gates_ref[...] = gates
    experts = gates.shape[1]
    total_rank = low.shape[1]
    rank = total_rank // experts
    spread = (
        lax.broadcasted_iota(jnp.int32, (experts, total_rank), 1) // rank
        == lax.broadcasted_iota(jnp.int32, (experts, total_rank), 0)
    ).astype(F32)
    loads[2].wait()
    low_b = dot(tok[...], down[...]).astype(BF16)
    low[...] = low_b
    wide_gates = dot(gates, spread, precision=lax.Precision.HIGHEST)
    mixed[...] = (low_b.astype(F32) * wide_gates).astype(BF16)
    dmix[...] = jnp.zeros_like(dmix)
    for copy in loads[3:]:
        copy.wait()

    def chunk_step(c, carry):
        for back in range(1, chips):
            j = z - back

            @pl.when(j >= 0)
            def _():
                to_next(c, j).wait_recv()

                @pl.when(z < chips - 1)
                def _():
                    to_next(c, j).start()

                to_mate(c, j).start()

        for back in range(chips):
            j = z - back

            @pl.when(j >= 0)
            def _():
                from_mate(c, j).wait_recv()

        cols = pl.ds(pl.multiple_of(c * wide, wide), wide)
        up_c = up[:, cols]
        query = (
            bq[:, cols].astype(F32) + ADAPTER_SCALE * dot(mixed[...], up_c)
        ).astype(BF16)
        cot_c = cot[:, cols]
        outs = []
        grads = []
        q_pos = core * rows + lax.broadcasted_iota(jnp.int32, (rows, 2 * rows), 0)
        visible = lax.broadcasted_iota(jnp.int32, (rows, 2 * rows), 1) <= q_pos
        qs = [query[:, h * HEAD_DIM : (h + 1) * HEAD_DIM] for h in range(heads)]
        cs = [cot_c[:, h * HEAD_DIM : (h + 1) * HEAD_DIM] for h in range(heads)]

        def block(j, states, masked):
            new_states = []
            for h in range(heads):
                hcols = slice(h * HEAD_DIM, (h + 1) * HEAD_DIM)
                keys = kv[c, j, :, 0, :, hcols].reshape(2 * rows, HEAD_DIM)
                values = kv[c, j, :, 1, :, hcols].reshape(2 * rows, HEAD_DIM)
                scores = dot(qs[h], keys, NT) * scale
                slopes = dot(cs[h], values, NT)
                if masked:
                    scores = jnp.where(visible, scores, MASKED)
                top = jnp.max(scores, axis=-1, keepdims=True)
                if states is not None:
                    old_top, old_sum, old_delta, old_vk, old_grad = states[h]
                    top = jnp.maximum(old_top, top)
                weights = jnp.exp(scores - top)
                products = weights * slopes
                total = jnp.sum(weights, axis=-1, keepdims=True)
                delta = jnp.sum(products, axis=-1, keepdims=True)
                vk = dot(weights.astype(BF16), jnp.concatenate([values, keys], axis=1))
                grad = dot(products.astype(BF16), keys)
                if states is not None:
                    fade = jnp.exp(old_top - top)
                    total = total + old_sum * fade
                    delta = delta + old_delta * fade
                    vk = vk + old_vk * fade
                    grad = grad + old_grad * fade
                new_states.append((top, total, delta, vk, grad))
            return tuple(new_states)

        states = block(z, None, True)
        states = lax.fori_loop(0, z, lambda j, st: block(j, st, False), states)
        for top, total, delta, vk, grad in states:
            inverse = 1.0 / total
            outs.append((vk[:, :HEAD_DIM] * inverse).astype(BF16))
            grads.append(
                (
                    scale
                    * (
                        grad * inverse
                        - (delta * inverse) * (vk[:, HEAD_DIM:] * inverse)
                    )
                ).astype(BF16)
            )
        out_ref[0, :, cols] = jnp.concatenate(outs, axis=1)
        dmix[...] += dot(jnp.concatenate(grads, axis=1), up_c, NT)
        return carry

    lax.fori_loop(0, chunks, chunk_step, 0)

    dgates = dot(
        ADAPTER_SCALE * dmix[...] * low[...].astype(F32), spread, NT,
        precision=lax.Precision.HIGHEST,
    )
    gates = gates_ref[...]
    dlogits = gates * (dgates - jnp.sum(gates * dgates, axis=-1, keepdims=True))
    partial = dot(dlogits.astype(BF16), tok[...], (((0,), (0,)), ((), ())))

    piece = part.shape[2]
    full = partial.shape[1]
    for n in range(n_seq):
        have = min(max(full - n * piece, 0), piece)
        if have:
            part[n, :, :have] = partial[:, n * piece : n * piece + have]
        if have < piece:
            part[n, :, have:] = jnp.zeros((part.shape[1], piece - have), F32)

    def exchange(axis, index, count, source, target, send, recv):
        copies = []
        for d in range(1, count):
            peer = lax.rem(index + d, count)
            copies.append(
                pltpu.make_async_remote_copy(
                    src_ref=source(peer), dst_ref=target.at[index],
                    send_sem=send.at[d], recv_sem=recv.at[index],
                    device_id={axis: peer}, device_id_type=MESH,
                )
            )
        for copy in copies:
            copy.start()
        for d in range(1, count):
            peer = lax.rem(index + d, count)
            pltpu.make_async_remote_copy(
                src_ref=source(peer), dst_ref=target.at[peer],
                send_sem=send.at[d], recv_sem=recv.at[peer],
                device_id={axis: peer}, device_id_type=MESH,
            ).wait_recv()
        return copies

    ra[me] = part[me]
    sent = exchange("seq", me, n_seq, lambda peer: part.at[peer], ra, a_send, a_recv)
    total = ra[0]
    for n in range(1, n_seq):
        total = total + ra[n]
    rb[dp] = total
    sent += exchange("dp", dp, n_dp, lambda peer: rb.at[dp], rb, b_send, b_recv)
    total = rb[0]
    for n in range(1, n_dp):
        total = total + rb[n]
    rc[me] = total
    sent += exchange("seq", me, n_seq, lambda peer: rc.at[me], rc, c_send, c_recv)
    for n in range(n_seq):
        have = min(max(full - n * piece, 0), piece)
        if have:
            gg_ref[:, n * piece : n * piece + have] = rc[n, :, :have]
    for copy in sent:
        copy.wait_send()

    def drain(c, carry):
        for back in range(chips):
            j = z - back

            @pl.when(j >= 0)
            def _():
                @pl.when(z < chips - 1)
                def _():
                    to_next(c, j).wait_send()

                to_mate(c, j).wait_send()

        return carry

    lax.fori_loop(0, chunks, drain, 0)


def shards(n_dp, n_seq, *args):
    tokens, base_query, k_base, v_base, cotangent, down, up, gate_weight = args
    rows, width = tokens.shape[1], base_query.shape[2]
    model, experts, total_rank = tokens.shape[2], gate_weight.shape[0], down.shape[1]
    head_count = width // HEAD_DIM
    heads = max(h for h in range(1, 5) if head_count % h == 0)
    chunks, chips = head_count // heads, n_seq // 2
    wide = heads * HEAD_DIM
    piece = -(-(model // 128) // n_seq) * 128
    any_spec = pl.BlockSpec(memory_space=pl.ANY)
    vmem_spec = pl.BlockSpec(memory_space=pltpu.VMEM)
    dma = pltpu.SemaphoreType.DMA
    return pl.pallas_call(
        functools.partial(kernel, chips, chunks, heads, n_dp),
        out_shape=(
            jax.ShapeDtypeStruct((1, rows, width), BF16),
            jax.ShapeDtypeStruct((experts, model), F32),
        ),
        in_specs=[any_spec] * 8,
        out_specs=(vmem_spec, vmem_spec),
        scratch_shapes=[
            pltpu.VMEM((chunks, chips, 2, 2, rows, wide), BF16),
            pltpu.VMEM((rows, width), BF16),
            pltpu.VMEM((rows, width), BF16),
            pltpu.VMEM((rows, model), BF16),
            pltpu.VMEM((model, total_rank), BF16),
            pltpu.VMEM((total_rank, width), BF16),
            pltpu.VMEM((experts, model), BF16),
            pltpu.VMEM((rows, total_rank), BF16),
            pltpu.VMEM((rows, total_rank), BF16),
            pltpu.VMEM((rows, total_rank), F32),
            pltpu.VMEM((rows, experts), F32),
            pltpu.VMEM((n_seq, experts, piece), F32),
            pltpu.VMEM((n_seq, experts, piece), F32),
            pltpu.VMEM((n_dp, experts, piece), F32),
            pltpu.VMEM((n_seq, experts, piece), F32),
            pltpu.VMEM((experts, piece), F32),
            dma((chunks, 2)),
            dma((6,)),
            dma((chunks, chips)),
            dma((chunks, chips)),
            dma((chunks, chips)),
            dma((chunks, chips)),
            dma((n_seq,)),
            dma((n_seq,)),
            dma((n_dp,)),
            dma((n_dp,)),
            dma((n_seq,)),
            dma((n_seq,)),
        ],
        compiler_params=pltpu.CompilerParams(
            collective_id=0, has_side_effects=True, vmem_limit_bytes=56 * 1024 * 1024
        ),
        cost_estimate=pl.CostEstimate(
            flops=10 * rows * rows * n_seq * width, bytes_accessed=16 * rows * width,
            transcendentals=rows * rows * n_seq * head_count,
        ),
    )(k_base, v_base, base_query, cotangent, tokens, down, up, gate_weight)


def solution(mesh):
    split = P("dp", "seq", None)
    return jax.shard_map(
        functools.partial(shards, mesh.shape["dp"], mesh.shape["seq"]),
        mesh=mesh,
        in_specs=(split, split, split, split, split, P(), P(), P()),
        out_specs=(split, P()),
        check_vma=False,
    )
```

```python
import functools

import jax
import jax.numpy as jnp
from jax import lax
from jax.experimental import pallas as pl
from jax.experimental.pallas import tpu as pltpu
from jax.sharding import PartitionSpec as P

HEAD_DIM = 128
ADAPTER_SCALE = 2.0
MASKED = -1e30
MESH = pl.DeviceIdType.MESH
F32 = jnp.float32
BF16 = jnp.bfloat16
NT = (((1,), (1,)), ((), ()))
NN = (((1,), (0,)), ((), ()))


def dot(a, b, dims=NN, precision=None):
    return lax.dot_general(a, b, dims, preferred_element_type=F32, precision=precision)


def kernel(
    chips, chunks, heads, n_dp,
    k_hbm, v_hbm, bq_hbm, cot_hbm, tok_hbm, down_hbm, up_hbm, gw_hbm,
    out_ref, gg_ref,
    kv, qb, ob, back, bq, tok, down, up, gw, low, dmix, gates_ref, part, ra, rb, rc,
    own_sem, load_sem, up_send, up_recv, mate_send, mate_recv,
    q_send, q_recv, ret_send, ret_recv,
    a_send, a_recv, b_send, b_recv, c_send, c_recv,
):
    n_seq = 2 * chips
    me = lax.axis_index("seq")
    dp = lax.axis_index("dp")
    z = me // 2
    core = lax.rem(me, 2)
    mate = me + 1 - 2 * core
    rows = tok.shape[0]
    wide = heads * HEAD_DIM
    scale = HEAD_DIM ** (-0.5)

    barrier = pltpu.get_barrier_semaphore()
    for d in range(1, n_seq):
        pl.semaphore_signal(
            barrier, inc=1, device_id={"seq": lax.rem(me + d, n_seq)}, device_id_type=MESH
        )
    for d in range(1, n_dp):
        pl.semaphore_signal(
            barrier, inc=1, device_id={"dp": lax.rem(dp + d, n_dp)}, device_id_type=MESH
        )

    def depth_of(c):
        return min(max(0, 2 - (c + 1) // 2), chips - 1)

    def own_copies(c):
        cols = pl.ds(c * wide, wide)
        return [
            pltpu.make_async_copy(src.at[0, :, cols], kv.at[c, z, core, i], own_sem.at[c, i])
            for i, src in enumerate((k_hbm, v_hbm))
        ]

    for c in range(chunks):
        for copy in own_copies(c):
            copy.start()
    loads = [
        pltpu.make_async_copy(src, dst, load_sem.at[i])
        for i, (src, dst) in enumerate(
            (
                (tok_hbm.at[0], tok), (gw_hbm, gw), (down_hbm, down), (up_hbm, up),
                (bq_hbm.at[0], bq),
            )
        )
    ] + [
        pltpu.make_async_copy(
            cot_hbm.at[0, :, pl.ds(c * wide, wide)], qb.at[c, 0, 1], load_sem.at[5 + c]
        )
        for c in range(chunks)
    ]
    for copy in loads:
        copy.start()
    pl.semaphore_wait(barrier, n_seq - 1 + n_dp - 1)

    def block_copy(c, j, side, send, recv, target):
        block = kv.at[c, j, side]
        return pltpu.make_async_remote_copy(
            src_ref=block, dst_ref=block, send_sem=send.at[c, j], recv_sem=recv.at[c, j],
            device_id={"seq": target}, device_id_type=MESH,
        )

    def to_next(c, j):
        return block_copy(c, j, core, up_send, up_recv, lax.rem(me + 2, n_seq))

    def to_mate(c, j):
        return block_copy(c, j, core, mate_send, mate_recv, mate)

    def from_mate(c, j):
        return block_copy(c, j, 1 - core, mate_send, mate_recv, mate)

    def host_of(c):
        return 2 * (chips - 1 - depth_of(c)) + core

    def to_host(c):
        return block_copy(c, z, core, up_send, up_recv, host_of(c))

    def query_to_host(c, d):
        return pltpu.make_async_remote_copy(
            src_ref=qb.at[c, 0], dst_ref=qb.at[c, d], send_sem=q_send.at[c],
            recv_sem=q_recv.at[c, d], device_id={"seq": host_of(c)}, device_id_type=MESH,
        )

    def give_back(c, d):
        return pltpu.make_async_remote_copy(
            src_ref=ob.at[c, d], dst_ref=back.at[c], send_sem=ret_send.at[c, d],
            recv_sem=ret_recv.at[c], device_id={"seq": lax.rem(me + 2 * d, n_seq)},
            device_id_type=MESH,
        )

    for c in range(chunks):
        host = chips - 1 - depth_of(c)
        for copy in own_copies(c):
            copy.wait()

        @pl.when(z < host)
        def _():
            to_next(c, z).start()

        @pl.when(z <= host)
        def _():
            to_mate(c, z).start()

        @pl.when(z > host)
        def _():
            to_host(c).start()

    loads[0].wait()
    loads[1].wait()
    logits = dot(tok[...], gw[...], NT)
    logits = jnp.exp(logits - jnp.max(logits, axis=-1, keepdims=True))
    gates = logits / jnp.sum(logits, axis=-1, keepdims=True)
    gates_ref[...] = gates
    experts = gates.shape[1]
    total_rank = low.shape[1]
    rank = total_rank // experts
    spread = (
        lax.broadcasted_iota(jnp.int32, (experts, total_rank), 1) // rank
        == lax.broadcasted_iota(jnp.int32, (experts, total_rank), 0)
    ).astype(F32)
    loads[2].wait()
    low_b = dot(tok[...], down[...]).astype(BF16)
    low[...] = low_b
    wide_gates = dot(gates, spread, precision=lax.Precision.HIGHEST)
    mixed = (low_b.astype(F32) * wide_gates).astype(BF16)
    dmix[...] = jnp.zeros_like(dmix)
    for copy in loads[3:]:
        copy.wait()
    for c in range(chunks):
        cols = slice(c * wide, (c + 1) * wide)
        qb[c, 0, 0] = (
            bq[:, cols].astype(F32) + ADAPTER_SCALE * dot(mixed, up[:, cols])
        ).astype(BF16)
        for d in range(1, depth_of(c) + 1):

            @pl.when(z == chips - 1 - depth_of(c) + d)
            def _():
                query_to_host(c, d).start()

    def attend(c, d):
        cols = slice(c * wide, (c + 1) * wide)
        q_pos = core * rows + lax.broadcasted_iota(jnp.int32, (rows, 2 * rows), 0)
        visible = lax.broadcasted_iota(jnp.int32, (rows, 2 * rows), 1) <= q_pos
        heads_at = [slice(h * HEAD_DIM, (h + 1) * HEAD_DIM) for h in range(heads)]

        def block(j, states, masked):
            new_states = []
            for h in range(heads):
                hcols = heads_at[h]
                keys = kv[c, j, :, 0, :, hcols].reshape(2 * rows, HEAD_DIM)
                values = kv[c, j, :, 1, :, hcols].reshape(2 * rows, HEAD_DIM)
                scores = dot(qb[c, d, 0, :, hcols], keys, NT) * scale
                slopes = dot(qb[c, d, 1, :, hcols], values, NT)
                if masked:
                    scores = jnp.where(visible, scores, MASKED)
                top = jnp.max(scores, axis=-1, keepdims=True)
                if states is not None:
                    old_top, old_sum, old_delta, old_vk, old_grad = states[h]
                    top = jnp.maximum(old_top, top)
                weights = jnp.exp(scores - top)
                products = weights * slopes
                total = jnp.sum(weights, axis=-1, keepdims=True)
                delta = jnp.sum(products, axis=-1, keepdims=True)
                vk = dot(weights.astype(BF16), jnp.concatenate([values, keys], axis=1))
                grad = dot(products.astype(BF16), keys)
                if states is not None:
                    fade = jnp.exp(old_top - top)
                    total = total + old_sum * fade
                    delta = delta + old_delta * fade
                    vk = vk + old_vk * fade
                    grad = grad + old_grad * fade
                new_states.append((top, total, delta, vk, grad))
            return tuple(new_states)

        states = block(z + d, None, True)
        states = lax.fori_loop(0, z + d, lambda j, st: block(j, st, False), states)
        outs = []
        grads = []
        for top, total, delta, vk, grad in states:
            inverse = 1.0 / total
            outs.append((vk[:, :HEAD_DIM] * inverse).astype(BF16))
            grads.append(
                (
                    scale
                    * (
                        grad * inverse
                        - (delta * inverse) * (vk[:, HEAD_DIM:] * inverse)
                    )
                ).astype(BF16)
            )
        return (
            jnp.concatenate(outs, axis=1),
            dot(jnp.concatenate(grads, axis=1), up[:, cols], NT),
        )

    def own_step(c):
        host = chips - 1 - depth_of(c)
        for gap in range(1, host + 1):

            @pl.when((z >= gap) & (z <= host))
            def _():
                to_next(c, z - gap).wait_recv()

                @pl.when(z < host)
                def _():
                    to_next(c, z - gap).start()

                to_mate(c, z - gap).start()

        @pl.when(z <= host)
        def _():
            def arrive(gap, carry):
                from_mate(c, z - gap).wait_recv()
                return carry

            lax.fori_loop(0, z + 1, arrive, 0)
            attended, term = attend(c, 0)
            out_ref[0, :, c * wide : (c + 1) * wide] = attended
            dmix[...] += term

    def hosted_step(c):
        host = chips - 1 - depth_of(c)

        @pl.when(z == host)
        def _():
            for d in range(1, depth_of(c) + 1):
                to_next(c, z + d).wait_recv()
                to_mate(c, z + d).start()
            for d in range(1, depth_of(c) + 1):
                from_mate(c, z + d).wait_recv()
                query_to_host(c, d).wait_recv()
                attended, term = attend(c, d)
                ob[c, d, :, :wide] = attended
                ob[c, d, :, wide:] = term.astype(BF16)
                give_back(c, d).start()

    deep = [c for c in range(chunks) if depth_of(c) > 1]
    waiting = []
    for c in range(chunks):
        own_step(c)
        if c == chunks - 1:
            waiting += deep
        for late in waiting:
            hosted_step(late)
        waiting = [c] if depth_of(c) == 1 else []
    for late in waiting:
        hosted_step(late)

    for c in range(chunks):
        if depth_of(c):

            @pl.when(z > chips - 1 - depth_of(c))
            def _():
                give_back(c, 1).wait_recv()
                out_ref[0, :, c * wide : (c + 1) * wide] = back[c, :, :wide]
                dmix[...] += back[c, :, wide:].astype(F32)

    dgates = dot(
        ADAPTER_SCALE * dmix[...] * low[...].astype(F32), spread, NT,
        precision=lax.Precision.HIGHEST,
    )
    gates = gates_ref[...]
    dlogits = gates * (dgates - jnp.sum(gates * dgates, axis=-1, keepdims=True))
    partial = dot(dlogits.astype(BF16), tok[...], (((0,), (0,)), ((), ())))

    piece = part.shape[2]
    full = partial.shape[1]
    for n in range(n_seq):
        have = min(max(full - n * piece, 0), piece)
        if have:
            part[n, :, :have] = partial[:, n * piece : n * piece + have]
        if have < piece:
            part[n, :, have:] = jnp.zeros((part.shape[1], piece - have), F32)

    def exchange(axis, index, count, source, target, send, recv):
        copies = []
        for d in range(1, count):
            peer = lax.rem(index + d, count)
            copies.append(
                pltpu.make_async_remote_copy(
                    src_ref=source(peer), dst_ref=target.at[index],
                    send_sem=send.at[d], recv_sem=recv.at[index],
                    device_id={axis: peer}, device_id_type=MESH,
                )
            )
        for copy in copies:
            copy.start()
        for d in range(1, count):
            peer = lax.rem(index + d, count)
            pltpu.make_async_remote_copy(
                src_ref=source(peer), dst_ref=target.at[peer],
                send_sem=send.at[d], recv_sem=recv.at[peer],
                device_id={axis: peer}, device_id_type=MESH,
            ).wait_recv()
        return copies

    ra[me] = part[me]
    sent = exchange("seq", me, n_seq, lambda peer: part.at[peer], ra, a_send, a_recv)
    total = ra[0]
    for n in range(1, n_seq):
        total = total + ra[n]
    rb[dp] = total
    sent += exchange("dp", dp, n_dp, lambda peer: rb.at[dp], rb, b_send, b_recv)
    total = rb[0]
    for n in range(1, n_dp):
        total = total + rb[n]
    rc[me] = total
    sent += exchange("seq", me, n_seq, lambda peer: rc.at[me], rc, c_send, c_recv)
    for n in range(n_seq):
        have = min(max(full - n * piece, 0), piece)
        if have:
            gg_ref[:, n * piece : n * piece + have] = rc[n, :, :have]
    for copy in sent:
        copy.wait_send()

    for c in range(chunks):
        depth = depth_of(c)
        host = chips - 1 - depth

        def drain(j, carry):
            @pl.when(z < host)
            def _():
                to_next(c, j).wait_send()

            to_mate(c, j).wait_send()
            return carry

        @pl.when(z <= host)
        def _():
            lax.fori_loop(0, z + 1, drain, 0)

        if depth:

            @pl.when(z == host)
            def _():
                for d in range(1, depth + 1):
                    to_mate(c, z + d).wait_send()
                    give_back(c, d).wait_send()

            @pl.when(z > host)
            def _():
                to_host(c).wait_send()
                query_to_host(c, 1).wait_send()


def shards(n_dp, n_seq, *args):
    tokens, base_query, k_base, v_base, cotangent, down, up, gate_weight = args
    rows, width = tokens.shape[1], base_query.shape[2]
    model, experts, total_rank = tokens.shape[2], gate_weight.shape[0], down.shape[1]
    head_count = width // HEAD_DIM
    heads = max(h for h in range(1, 5) if head_count % h == 0)
    chunks, chips = head_count // heads, n_seq // 2
    wide = heads * HEAD_DIM
    piece = -(-(model // 128) // n_seq) * 128
    any_spec = pl.BlockSpec(memory_space=pl.ANY)
    vmem_spec = pl.BlockSpec(memory_space=pltpu.VMEM)
    dma = pltpu.SemaphoreType.DMA
    return pl.pallas_call(
        functools.partial(kernel, chips, chunks, heads, n_dp),
        out_shape=(
            jax.ShapeDtypeStruct((1, rows, width), BF16),
            jax.ShapeDtypeStruct((experts, model), F32),
        ),
        in_specs=[any_spec] * 8,
        out_specs=(vmem_spec, vmem_spec),
        scratch_shapes=[
            pltpu.VMEM((chunks, chips, 2, 2, rows, wide), BF16),
            pltpu.VMEM((chunks, 3, 2, rows, wide), BF16),
            pltpu.VMEM((chunks, 3, rows, wide + total_rank), BF16),
            pltpu.VMEM((chunks, rows, wide + total_rank), BF16),
            pltpu.VMEM((rows, width), BF16),
            pltpu.VMEM((rows, model), BF16),
            pltpu.VMEM((model, total_rank), BF16),
            pltpu.VMEM((total_rank, width), BF16),
            pltpu.VMEM((experts, model), BF16),
            pltpu.VMEM((rows, total_rank), BF16),
            pltpu.VMEM((rows, total_rank), F32),
            pltpu.VMEM((rows, experts), F32),
            pltpu.VMEM((n_seq, experts, piece), F32),
            pltpu.VMEM((n_seq, experts, piece), F32),
            pltpu.VMEM((n_dp, experts, piece), F32),
            pltpu.VMEM((n_seq, experts, piece), F32),
            dma((chunks, 2)),
            dma((5 + chunks,)),
            dma((chunks, chips)),
            dma((chunks, chips)),
            dma((chunks, chips)),
            dma((chunks, chips)),
            dma((chunks,)),
            dma((chunks, 3)),
            dma((chunks, 3)),
            dma((chunks,)),
            dma((n_seq,)),
            dma((n_seq,)),
            dma((n_dp,)),
            dma((n_dp,)),
            dma((n_seq,)),
            dma((n_seq,)),
        ],
        compiler_params=pltpu.CompilerParams(
            collective_id=0, has_side_effects=True, vmem_limit_bytes=56 * 1024 * 1024
        ),
        cost_estimate=pl.CostEstimate(
            flops=10 * rows * rows * n_seq * width, bytes_accessed=16 * rows * width,
            transcendentals=rows * rows * n_seq * head_count,
        ),
    )(k_base, v_base, base_query, cotangent, tokens, down, up, gate_weight)


def solution(mesh):
    split = P("dp", "seq", None)
    return jax.shard_map(
        functools.partial(shards, mesh.shape["dp"], mesh.shape["seq"]),
        mesh=mesh,
        in_specs=(split, split, split, split, split, P(), P(), P()),
        out_specs=(split, P()),
        check_vma=False,
    )
```

```python
import functools

import jax
import jax.numpy as jnp
from jax import lax
from jax.experimental import pallas as pl
from jax.experimental.pallas import tpu as pltpu
from jax.sharding import PartitionSpec as P

HEAD_DIM = 128
ADAPTER_SCALE = 2.0
MASKED = -1e30
MESH = pl.DeviceIdType.MESH
F32 = jnp.float32
BF16 = jnp.bfloat16
NT = (((1,), (1,)), ((), ()))
NN = (((1,), (0,)), ((), ()))


def dot(a, b, dims=NN, precision=None):
    return lax.dot_general(a, b, dims, preferred_element_type=F32, precision=precision)


def kernel(
    chips, chunks, heads, n_dp,
    k_hbm, v_hbm, bq_hbm, cot_hbm, tok_hbm, down_hbm, up_hbm, gw_hbm,
    out_ref, gg_ref,
    kv, qb, ob, back, sc, peak, bq, tok, down, up, gw, low, dmix, gates_ref, part, ra, rb, rc,
    own_sem, load_sem, up_send, up_recv, mate_send, mate_recv,
    q_send, q_recv, ret_send, ret_recv,
    a_send, a_recv, b_send, b_recv, c_send, c_recv,
):
    n_seq = 2 * chips
    me = lax.axis_index("seq")
    dp = lax.axis_index("dp")
    z = me // 2
    core = lax.rem(me, 2)
    mate = me + 1 - 2 * core
    rows = tok.shape[0]
    wide = heads * HEAD_DIM
    scale = HEAD_DIM ** (-0.5)

    barrier = pltpu.get_barrier_semaphore()
    for d in range(1, n_seq):
        pl.semaphore_signal(
            barrier, inc=1, device_id={"seq": lax.rem(me + d, n_seq)}, device_id_type=MESH
        )
    for d in range(1, n_dp):
        pl.semaphore_signal(
            barrier, inc=1, device_id={"dp": lax.rem(dp + d, n_dp)}, device_id_type=MESH
        )

    def depth_of(c):
        return min(max(0, 2 - (c + 1) // 2), chips - 1)

    def own_copies(c):
        cols = pl.ds(c * wide, wide)
        return [
            pltpu.make_async_copy(src.at[0, :, cols], kv.at[c, z, core, i], own_sem.at[c, i])
            for i, src in enumerate((k_hbm, v_hbm))
        ]

    for c in range(chunks):
        for copy in own_copies(c):
            copy.start()
    loads = [
        pltpu.make_async_copy(src, dst, load_sem.at[i])
        for i, (src, dst) in enumerate(
            (
                (tok_hbm.at[0], tok), (gw_hbm, gw), (down_hbm, down), (up_hbm, up),
                (bq_hbm.at[0], bq),
            )
        )
    ] + [
        pltpu.make_async_copy(
            cot_hbm.at[0, :, pl.ds(c * wide, wide)], qb.at[c, 0, 1], load_sem.at[5 + c]
        )
        for c in range(chunks)
    ]
    for copy in loads:
        copy.start()
    pl.semaphore_wait(barrier, n_seq - 1 + n_dp - 1)

    def block_copy(c, j, side, send, recv, target):
        block = kv.at[c, j, side]
        return pltpu.make_async_remote_copy(
            src_ref=block, dst_ref=block, send_sem=send.at[c, j], recv_sem=recv.at[c, j],
            device_id={"seq": target}, device_id_type=MESH,
        )

    def to_next(c, j):
        return block_copy(c, j, core, up_send, up_recv, lax.rem(me + 2, n_seq))

    def to_mate(c, j):
        return block_copy(c, j, core, mate_send, mate_recv, mate)

    def from_mate(c, j):
        return block_copy(c, j, 1 - core, mate_send, mate_recv, mate)

    def host_of(c):
        return 2 * (chips - 1 - depth_of(c)) + core

    def to_host(c):
        return block_copy(c, z, core, up_send, up_recv, host_of(c))

    def query_to_host(c, d):
        return pltpu.make_async_remote_copy(
            src_ref=qb.at[c, 0], dst_ref=qb.at[c, d], send_sem=q_send.at[c],
            recv_sem=q_recv.at[c, d], device_id={"seq": host_of(c)}, device_id_type=MESH,
        )

    def give_back(c, d):
        return pltpu.make_async_remote_copy(
            src_ref=ob.at[c, d], dst_ref=back.at[c], send_sem=ret_send.at[c, d],
            recv_sem=ret_recv.at[c], device_id={"seq": lax.rem(me + 2 * d, n_seq)},
            device_id_type=MESH,
        )

    for c in range(chunks):
        host = chips - 1 - depth_of(c)
        for copy in own_copies(c):
            copy.wait()

        @pl.when(z < host)
        def _():
            to_next(c, z).start()

        @pl.when(z <= host)
        def _():
            to_mate(c, z).start()

        @pl.when(z > host)
        def _():
            to_host(c).start()

    loads[0].wait()
    loads[1].wait()
    logits = dot(tok[...], gw[...], NT)
    logits = jnp.exp(logits - jnp.max(logits, axis=-1, keepdims=True))
    gates = logits / jnp.sum(logits, axis=-1, keepdims=True)
    gates_ref[...] = gates
    experts = gates.shape[1]
    total_rank = low.shape[1]
    rank = total_rank // experts
    spread = (
        lax.broadcasted_iota(jnp.int32, (experts, total_rank), 1) // rank
        == lax.broadcasted_iota(jnp.int32, (experts, total_rank), 0)
    ).astype(F32)
    loads[2].wait()
    low_b = dot(tok[...], down[...]).astype(BF16)
    low[...] = low_b
    wide_gates = dot(gates, spread, precision=lax.Precision.HIGHEST)
    mixed = (low_b.astype(F32) * wide_gates).astype(BF16)
    dmix[...] = jnp.zeros_like(dmix)
    for copy in loads[3:]:
        copy.wait()
    for c in range(chunks):
        cols = slice(c * wide, (c + 1) * wide)
        qb[c, 0, 0] = (
            bq[:, cols].astype(F32) + ADAPTER_SCALE * dot(mixed, up[:, cols])
        ).astype(BF16)
        for d in range(1, depth_of(c) + 1):

            @pl.when(z == chips - 1 - depth_of(c) + d)
            def _():
                query_to_host(c, d).start()

    def attend(c, d):
        cols = slice(c * wide, (c + 1) * wide)
        q_pos = core * rows + lax.broadcasted_iota(jnp.int32, (rows, 2 * rows), 0)
        visible = lax.broadcasted_iota(jnp.int32, (rows, 2 * rows), 1) <= q_pos
        heads_at = [slice(h * HEAD_DIM, (h + 1) * HEAD_DIM) for h in range(heads)]

        def fold(x, op):
            return op(x[:, :rows], x[:, rows:])

        last = z + d

        def score(j, h):
            keys = kv[c, j, :, 0, :, heads_at[h]].reshape(2 * rows, HEAD_DIM)
            return dot(qb[c, d, 0, :, heads_at[h]], keys, NT) * scale

        tops = []
        for h in range(heads):
            found = jnp.where(visible, score(last, h), MASKED)
            sc[h, last] = found
            tops.append(fold(found, jnp.maximum))

        def first_pass(j, tops):
            new_tops = []
            for h in range(heads):
                found = score(j, h)
                sc[h, j] = found
                new_tops.append(jnp.maximum(tops[h], fold(found, jnp.maximum)))
            return tuple(new_tops)

        tops = lax.fori_loop(0, last, first_pass, tuple(tops))
        for h in range(heads):
            peak[h] = jnp.broadcast_to(
                jnp.max(tops[h], axis=-1, keepdims=True), (rows, rows)
            )

        def second_pass(j, states):
            new_states = []
            for h in range(heads):
                total, delta, vk, grad = states[h]
                keys = kv[c, j, :, 0, :, heads_at[h]].reshape(2 * rows, HEAD_DIM)
                values = kv[c, j, :, 1, :, heads_at[h]].reshape(2 * rows, HEAD_DIM)
                slopes = dot(qb[c, d, 1, :, heads_at[h]], values, NT)
                top = peak[h]
                weights = jnp.exp(sc[h, j] - jnp.concatenate([top, top], axis=1))
                products = weights * slopes
                new_states.append(
                    (
                        total + fold(weights, jnp.add),
                        delta + fold(products, jnp.add),
                        vk + dot(weights.astype(BF16), jnp.concatenate([values, keys], axis=1)),
                        grad + dot(products.astype(BF16), keys),
                    )
                )
            return tuple(new_states)

        empty = jnp.zeros((rows, rows), F32)
        zero = jnp.zeros((rows, HEAD_DIM), F32)
        zeros = jnp.zeros((rows, 2 * HEAD_DIM), F32)
        states = lax.fori_loop(
            0, last + 1, second_pass, ((empty, empty, zeros, zero),) * heads
        )
        outs = []
        grads = []
        for total, delta, vk, grad in states:
            inverse = 1.0 / jnp.sum(total, axis=-1, keepdims=True)
            delta = jnp.sum(delta, axis=-1, keepdims=True)
            outs.append((vk[:, :HEAD_DIM] * inverse).astype(BF16))
            grads.append(
                (
                    scale
                    * (
                        grad * inverse
                        - (delta * inverse) * (vk[:, HEAD_DIM:] * inverse)
                    )
                ).astype(BF16)
            )
        return (
            jnp.concatenate(outs, axis=1),
            dot(jnp.concatenate(grads, axis=1), up[:, cols], NT),
        )

    def own_step(c):
        host = chips - 1 - depth_of(c)
        for gap in range(1, host + 1):

            @pl.when((z >= gap) & (z <= host))
            def _():
                to_next(c, z - gap).wait_recv()

                @pl.when(z < host)
                def _():
                    to_next(c, z - gap).start()

                to_mate(c, z - gap).start()

        @pl.when(z <= host)
        def _():
            def arrive(gap, carry):
                from_mate(c, z - gap).wait_recv()
                return carry

            lax.fori_loop(0, z + 1, arrive, 0)
            attended, term = attend(c, 0)
            out_ref[0, :, c * wide : (c + 1) * wide] = attended
            dmix[...] += term

    def hosted_step(c):
        host = chips - 1 - depth_of(c)

        @pl.when(z == host)
        def _():
            for d in range(1, depth_of(c) + 1):
                to_next(c, z + d).wait_recv()
                to_mate(c, z + d).start()
            for d in range(1, depth_of(c) + 1):
                from_mate(c, z + d).wait_recv()
                query_to_host(c, d).wait_recv()
                attended, term = attend(c, d)
                ob[c, d, :, :wide] = attended
                ob[c, d, :, wide:] = term.astype(BF16)
                give_back(c, d).start()

    deep = [c for c in range(chunks) if depth_of(c) > 1]
    waiting = []
    for c in range(chunks):
        own_step(c)
        if c == chunks - 1:
            waiting += deep
        for late in waiting:
            hosted_step(late)
        waiting = [c] if depth_of(c) == 1 else []
    for late in waiting:
        hosted_step(late)

    for c in range(chunks):
        if depth_of(c):

            @pl.when(z > chips - 1 - depth_of(c))
            def _():
                give_back(c, 1).wait_recv()
                out_ref[0, :, c * wide : (c + 1) * wide] = back[c, :, :wide]
                dmix[...] += back[c, :, wide:].astype(F32)

    dgates = dot(
        ADAPTER_SCALE * dmix[...] * low[...].astype(F32), spread, NT,
        precision=lax.Precision.HIGHEST,
    )
    gates = gates_ref[...]
    dlogits = gates * (dgates - jnp.sum(gates * dgates, axis=-1, keepdims=True))
    partial = dot(dlogits.astype(BF16), tok[...], (((0,), (0,)), ((), ())))

    piece = part.shape[2]
    full = partial.shape[1]
    for n in range(n_seq):
        have = min(max(full - n * piece, 0), piece)
        if have:
            part[n, :, :have] = partial[:, n * piece : n * piece + have]
        if have < piece:
            part[n, :, have:] = jnp.zeros((part.shape[1], piece - have), F32)

    def exchange(axis, index, count, source, target, send, recv):
        copies = []
        for d in range(1, count):
            peer = lax.rem(index + d, count)
            copies.append(
                pltpu.make_async_remote_copy(
                    src_ref=source(peer), dst_ref=target.at[index],
                    send_sem=send.at[d], recv_sem=recv.at[index],
                    device_id={axis: peer}, device_id_type=MESH,
                )
            )
        for copy in copies:
            copy.start()
        for d in range(1, count):
            peer = lax.rem(index + d, count)
            pltpu.make_async_remote_copy(
                src_ref=source(peer), dst_ref=target.at[peer],
                send_sem=send.at[d], recv_sem=recv.at[peer],
                device_id={axis: peer}, device_id_type=MESH,
            ).wait_recv()
        return copies

    ra[me] = part[me]
    sent = exchange("seq", me, n_seq, lambda peer: part.at[peer], ra, a_send, a_recv)
    total = ra[0]
    for n in range(1, n_seq):
        total = total + ra[n]
    rb[dp] = total
    sent += exchange("dp", dp, n_dp, lambda peer: rb.at[dp], rb, b_send, b_recv)
    total = rb[0]
    for n in range(1, n_dp):
        total = total + rb[n]
    rc[me] = total
    sent += exchange("seq", me, n_seq, lambda peer: rc.at[me], rc, c_send, c_recv)
    for n in range(n_seq):
        have = min(max(full - n * piece, 0), piece)
        if have:
            gg_ref[:, n * piece : n * piece + have] = rc[n, :, :have]
    for copy in sent:
        copy.wait_send()

    for c in range(chunks):
        depth = depth_of(c)
        host = chips - 1 - depth

        def drain(j, carry):
            @pl.when(z < host)
            def _():
                to_next(c, j).wait_send()

            to_mate(c, j).wait_send()
            return carry

        @pl.when(z <= host)
        def _():
            lax.fori_loop(0, z + 1, drain, 0)

        if depth:

            @pl.when(z == host)
            def _():
                for d in range(1, depth + 1):
                    to_mate(c, z + d).wait_send()
                    give_back(c, d).wait_send()

            @pl.when(z > host)
            def _():
                to_host(c).wait_send()
                query_to_host(c, 1).wait_send()


def shards(n_dp, n_seq, *args):
    tokens, base_query, k_base, v_base, cotangent, down, up, gate_weight = args
    rows, width = tokens.shape[1], base_query.shape[2]
    model, experts, total_rank = tokens.shape[2], gate_weight.shape[0], down.shape[1]
    head_count = width // HEAD_DIM
    heads = max(h for h in range(1, 5) if head_count % h == 0)
    chunks, chips = head_count // heads, n_seq // 2
    wide = heads * HEAD_DIM
    piece = -(-(model // 128) // n_seq) * 128
    any_spec = pl.BlockSpec(memory_space=pl.ANY)
    vmem_spec = pl.BlockSpec(memory_space=pltpu.VMEM)
    dma = pltpu.SemaphoreType.DMA
    return pl.pallas_call(
        functools.partial(kernel, chips, chunks, heads, n_dp),
        out_shape=(
            jax.ShapeDtypeStruct((1, rows, width), BF16),
            jax.ShapeDtypeStruct((experts, model), F32),
        ),
        in_specs=[any_spec] * 8,
        out_specs=(vmem_spec, vmem_spec),
        scratch_shapes=[
            pltpu.VMEM((chunks, chips, 2, 2, rows, wide), BF16),
            pltpu.VMEM((chunks, 3, 2, rows, wide), BF16),
            pltpu.VMEM((chunks, 3, rows, wide + total_rank), BF16),
            pltpu.VMEM((chunks, rows, wide + total_rank), BF16),
            pltpu.VMEM((heads, chips, rows, 2 * rows), F32),
            pltpu.VMEM((heads, rows, rows), F32),
            pltpu.VMEM((rows, width), BF16),
            pltpu.VMEM((rows, model), BF16),
            pltpu.VMEM((model, total_rank), BF16),
            pltpu.VMEM((total_rank, width), BF16),
            pltpu.VMEM((experts, model), BF16),
            pltpu.VMEM((rows, total_rank), BF16),
            pltpu.VMEM((rows, total_rank), F32),
            pltpu.VMEM((rows, experts), F32),
            pltpu.VMEM((n_seq, experts, piece), F32),
            pltpu.VMEM((n_seq, experts, piece), F32),
            pltpu.VMEM((n_dp, experts, piece), F32),
            pltpu.VMEM((n_seq, experts, piece), F32),
            dma((chunks, 2)),
            dma((5 + chunks,)),
            dma((chunks, chips)),
            dma((chunks, chips)),
            dma((chunks, chips)),
            dma((chunks, chips)),
            dma((chunks,)),
            dma((chunks, 3)),
            dma((chunks, 3)),
            dma((chunks,)),
            dma((n_seq,)),
            dma((n_seq,)),
            dma((n_dp,)),
            dma((n_dp,)),
            dma((n_seq,)),
            dma((n_seq,)),
        ],
        compiler_params=pltpu.CompilerParams(
            collective_id=0, has_side_effects=True, vmem_limit_bytes=56 * 1024 * 1024
        ),
        cost_estimate=pl.CostEstimate(
            flops=10 * rows * rows * n_seq * width, bytes_accessed=16 * rows * width,
            transcendentals=rows * rows * n_seq * head_count,
        ),
    )(k_base, v_base, base_query, cotangent, tokens, down, up, gate_weight)


def solution(mesh):
    split = P("dp", "seq", None)
    return jax.shard_map(
        functools.partial(shards, mesh.shape["dp"], mesh.shape["seq"]),
        mesh=mesh,
        in_specs=(split, split, split, split, split, P(), P(), P()),
        out_specs=(split, P()),
        check_vma=False,
    )
```

```python
import functools

import jax
import jax.numpy as jnp
from jax import lax
from jax.experimental import pallas as pl
from jax.experimental.pallas import tpu as pltpu
from jax.sharding import PartitionSpec as P

HEAD_DIM = 128
ADAPTER_SCALE = 2.0
MASKED = -1e30
MESH = pl.DeviceIdType.MESH
F32 = jnp.float32
BF16 = jnp.bfloat16
NT = (((1,), (1,)), ((), ()))
NN = (((1,), (0,)), ((), ()))


def dot(a, b, dims=NN, precision=None):
    return lax.dot_general(a, b, dims, preferred_element_type=F32, precision=precision)


def kernel(
    chips, chunks, heads, n_dp,
    k_hbm, v_hbm, bq_hbm, cot_hbm, tok_hbm, down_hbm, up_hbm, gw_hbm,
    out_ref, gg_ref,
    kv, qb, ob, back, sc, peak, bq, tok, down, up, gw, low, dmix, gates_ref, part, ra, rb, rc,
    own_sem, load_sem, up_send, up_recv, mate_send, mate_recv,
    q_send, q_recv, ret_send, ret_recv,
    a_send, a_recv, b_send, b_recv, c_send, c_recv,
):
    n_seq = 2 * chips
    me = lax.axis_index("seq")
    dp = lax.axis_index("dp")
    z = me // 2
    core = lax.rem(me, 2)
    mate = me + 1 - 2 * core
    rows = tok.shape[0]
    wide = heads * HEAD_DIM
    scale = HEAD_DIM ** (-0.5)

    barrier = pltpu.get_barrier_semaphore()
    for d in range(1, n_seq):
        pl.semaphore_signal(
            barrier, inc=1, device_id={"seq": lax.rem(me + d, n_seq)}, device_id_type=MESH
        )
    for d in range(1, n_dp):
        pl.semaphore_signal(
            barrier, inc=1, device_id={"dp": lax.rem(dp + d, n_dp)}, device_id_type=MESH
        )

    def depth_of(c):
        return min(1 if c < chunks // 2 else 0, chips - 1)

    def own_copies(c):
        cols = pl.ds(c * wide, wide)
        return [
            pltpu.make_async_copy(src.at[0, :, cols], kv.at[c, z, core, i], own_sem.at[c, i])
            for i, src in enumerate((k_hbm, v_hbm))
        ]

    for c in range(chunks):
        for copy in own_copies(c):
            copy.start()
    loads = [
        pltpu.make_async_copy(src, dst, load_sem.at[i])
        for i, (src, dst) in enumerate(
            (
                (tok_hbm.at[0], tok), (gw_hbm, gw), (down_hbm, down), (up_hbm, up),
                (bq_hbm.at[0], bq),
            )
        )
    ] + [
        pltpu.make_async_copy(
            cot_hbm.at[0, :, pl.ds(c * wide, wide)], qb.at[c, 0, 1], load_sem.at[5 + c]
        )
        for c in range(chunks)
    ]
    for copy in loads:
        copy.start()
    pl.semaphore_wait(barrier, n_seq - 1 + n_dp - 1)

    def block_copy(c, j, side, send, recv, target):
        block = kv.at[c, j, side]
        return pltpu.make_async_remote_copy(
            src_ref=block, dst_ref=block, send_sem=send.at[c, j], recv_sem=recv.at[c, j],
            device_id={"seq": target}, device_id_type=MESH,
        )

    def to_next(c, j):
        return block_copy(c, j, core, up_send, up_recv, lax.rem(me + 2, n_seq))

    def to_mate(c, j):
        return block_copy(c, j, core, mate_send, mate_recv, mate)

    def from_mate(c, j):
        return block_copy(c, j, 1 - core, mate_send, mate_recv, mate)

    def host_of(c):
        return 2 * (chips - 1 - depth_of(c)) + core

    def to_host(c):
        return block_copy(c, z, core, up_send, up_recv, host_of(c))

    def query_to_host(c, d):
        return pltpu.make_async_remote_copy(
            src_ref=qb.at[c, 0], dst_ref=qb.at[c, d], send_sem=q_send.at[c],
            recv_sem=q_recv.at[c, d], device_id={"seq": host_of(c)}, device_id_type=MESH,
        )

    def give_back(c, d):
        return pltpu.make_async_remote_copy(
            src_ref=ob.at[c, d], dst_ref=back.at[c], send_sem=ret_send.at[c, d],
            recv_sem=ret_recv.at[c], device_id={"seq": lax.rem(me + 2 * d, n_seq)},
            device_id_type=MESH,
        )

    for c in range(chunks):
        host = chips - 1 - depth_of(c)
        for copy in own_copies(c):
            copy.wait()

        @pl.when(z < host)
        def _():
            to_next(c, z).start()

        @pl.when(z <= host)
        def _():
            to_mate(c, z).start()

        @pl.when(z > host)
        def _():
            to_host(c).start()

    loads[0].wait()
    loads[1].wait()
    logits = dot(tok[...], gw[...], NT)
    logits = jnp.exp(logits - jnp.max(logits, axis=-1, keepdims=True))
    gates = logits / jnp.sum(logits, axis=-1, keepdims=True)
    gates_ref[...] = gates
    experts = gates.shape[1]
    total_rank = low.shape[1]
    rank = total_rank // experts
    spread = (
        lax.broadcasted_iota(jnp.int32, (experts, total_rank), 1) // rank
        == lax.broadcasted_iota(jnp.int32, (experts, total_rank), 0)
    ).astype(F32)
    loads[2].wait()
    low_b = dot(tok[...], down[...]).astype(BF16)
    low[...] = low_b
    wide_gates = dot(gates, spread, precision=lax.Precision.HIGHEST)
    mixed = (low_b.astype(F32) * wide_gates).astype(BF16)
    dmix[...] = jnp.zeros_like(dmix)
    for copy in loads[3:]:
        copy.wait()
    for c in range(chunks):
        cols = slice(c * wide, (c + 1) * wide)
        qb[c, 0, 0] = (
            bq[:, cols].astype(F32) + ADAPTER_SCALE * dot(mixed, up[:, cols])
        ).astype(BF16)
        for d in range(1, depth_of(c) + 1):

            @pl.when(z == chips - 1 - depth_of(c) + d)
            def _():
                query_to_host(c, d).start()

    def attend(c, d):
        cols = slice(c * wide, (c + 1) * wide)
        q_pos = core * rows + lax.broadcasted_iota(jnp.int32, (rows, 2 * rows), 0)
        visible = lax.broadcasted_iota(jnp.int32, (rows, 2 * rows), 1) <= q_pos
        heads_at = [slice(h * HEAD_DIM, (h + 1) * HEAD_DIM) for h in range(heads)]

        def fold(x, op):
            return op(x[:, :rows], x[:, rows:])

        last = z + d

        def score(j, h):
            keys = kv[c, j, :, 0, :, heads_at[h]].reshape(2 * rows, HEAD_DIM)
            return dot(qb[c, d, 0, :, heads_at[h]], keys, NT) * scale

        tops = []
        for h in range(heads):
            found = jnp.where(visible, score(last, h), MASKED)
            sc[h, last] = found
            tops.append(fold(found, jnp.maximum))

        def first_pass(j, tops):
            new_tops = []
            for h in range(heads):
                found = score(j, h)
                sc[h, j] = found
                new_tops.append(jnp.maximum(tops[h], fold(found, jnp.maximum)))
            return tuple(new_tops)

        tops = lax.fori_loop(0, last, first_pass, tuple(tops))
        for h in range(heads):
            peak[h] = jnp.broadcast_to(
                jnp.max(tops[h], axis=-1, keepdims=True), (rows, rows)
            )

        def second_pass(j, states):
            new_states = []
            for h in range(heads):
                total, delta, vk, grad = states[h]
                keys = kv[c, j, :, 0, :, heads_at[h]].reshape(2 * rows, HEAD_DIM)
                values = kv[c, j, :, 1, :, heads_at[h]].reshape(2 * rows, HEAD_DIM)
                slopes = dot(qb[c, d, 1, :, heads_at[h]], values, NT)
                top = peak[h]
                weights = jnp.exp(sc[h, j] - jnp.concatenate([top, top], axis=1))
                products = weights * slopes
                new_states.append(
                    (
                        total + fold(weights, jnp.add),
                        delta + fold(products, jnp.add),
                        vk + dot(weights.astype(BF16), jnp.concatenate([values, keys], axis=1)),
                        grad + dot(products.astype(BF16), keys),
                    )
                )
            return tuple(new_states)

        empty = jnp.zeros((rows, rows), F32)
        zero = jnp.zeros((rows, HEAD_DIM), F32)
        zeros = jnp.zeros((rows, 2 * HEAD_DIM), F32)
        states = lax.fori_loop(
            0, last + 1, second_pass, ((empty, empty, zeros, zero),) * heads
        )
        outs = []
        grads = []
        for total, delta, vk, grad in states:
            inverse = 1.0 / jnp.sum(total, axis=-1, keepdims=True)
            delta = jnp.sum(delta, axis=-1, keepdims=True)
            outs.append((vk[:, :HEAD_DIM] * inverse).astype(BF16))
            grads.append(
                (
                    scale
                    * (
                        grad * inverse
                        - (delta * inverse) * (vk[:, HEAD_DIM:] * inverse)
                    )
                ).astype(BF16)
            )
        return (
            jnp.concatenate(outs, axis=1),
            dot(jnp.concatenate(grads, axis=1), up[:, cols], NT),
        )

    def own_step(c):
        host = chips - 1 - depth_of(c)
        for gap in range(1, host + 1):

            @pl.when((z >= gap) & (z <= host))
            def _():
                to_next(c, z - gap).wait_recv()

                @pl.when(z < host)
                def _():
                    to_next(c, z - gap).start()

                to_mate(c, z - gap).start()

        @pl.when(z <= host)
        def _():
            def arrive(gap, carry):
                from_mate(c, z - gap).wait_recv()
                return carry

            lax.fori_loop(0, z + 1, arrive, 0)
            attended, term = attend(c, 0)
            out_ref[0, :, c * wide : (c + 1) * wide] = attended
            dmix[...] += term

    def hosted_step(c):
        host = chips - 1 - depth_of(c)

        @pl.when(z == host)
        def _():
            for d in range(1, depth_of(c) + 1):
                to_next(c, z + d).wait_recv()
                to_mate(c, z + d).start()
            for d in range(1, depth_of(c) + 1):
                from_mate(c, z + d).wait_recv()
                query_to_host(c, d).wait_recv()
                attended, term = attend(c, d)
                ob[c, d, :, :wide] = attended
                ob[c, d, :, wide:] = term.astype(BF16)
                give_back(c, d).start()

    deep = [c for c in range(chunks) if depth_of(c) > 1]
    waiting = []
    for c in range(chunks):
        own_step(c)
        if c == chunks - 1:
            waiting += deep
        for late in waiting:
            hosted_step(late)
        waiting = [c] if depth_of(c) == 1 else []
    for late in waiting:
        hosted_step(late)

    for c in range(chunks):
        if depth_of(c):

            @pl.when(z > chips - 1 - depth_of(c))
            def _():
                give_back(c, 1).wait_recv()
                out_ref[0, :, c * wide : (c + 1) * wide] = back[c, :, :wide]
                dmix[...] += back[c, :, wide:].astype(F32)

    dgates = dot(
        ADAPTER_SCALE * dmix[...] * low[...].astype(F32), spread, NT,
        precision=lax.Precision.HIGHEST,
    )
    gates = gates_ref[...]
    dlogits = gates * (dgates - jnp.sum(gates * dgates, axis=-1, keepdims=True))
    partial = dot(dlogits.astype(BF16), tok[...], (((0,), (0,)), ((), ())))

    piece = part.shape[2]
    full = partial.shape[1]
    for n in range(n_seq):
        have = min(max(full - n * piece, 0), piece)
        if have:
            part[n, :, :have] = partial[:, n * piece : n * piece + have]
        if have < piece:
            part[n, :, have:] = jnp.zeros((part.shape[1], piece - have), F32)

    def exchange(axis, index, count, source, target, send, recv):
        copies = []
        for d in range(1, count):
            peer = lax.rem(index + d, count)
            copies.append(
                pltpu.make_async_remote_copy(
                    src_ref=source(peer), dst_ref=target.at[index],
                    send_sem=send.at[d], recv_sem=recv.at[index],
                    device_id={axis: peer}, device_id_type=MESH,
                )
            )
        for copy in copies:
            copy.start()
        for d in range(1, count):
            peer = lax.rem(index + d, count)
            pltpu.make_async_remote_copy(
                src_ref=source(peer), dst_ref=target.at[peer],
                send_sem=send.at[d], recv_sem=recv.at[peer],
                device_id={axis: peer}, device_id_type=MESH,
            ).wait_recv()
        return copies

    ra[me] = part[me]
    sent = exchange("seq", me, n_seq, lambda peer: part.at[peer], ra, a_send, a_recv)
    total = ra[0]
    for n in range(1, n_seq):
        total = total + ra[n]
    rb[dp] = total
    sent += exchange("dp", dp, n_dp, lambda peer: rb.at[dp], rb, b_send, b_recv)
    total = rb[0]
    for n in range(1, n_dp):
        total = total + rb[n]
    rc[me] = total
    sent += exchange("seq", me, n_seq, lambda peer: rc.at[me], rc, c_send, c_recv)
    for n in range(n_seq):
        have = min(max(full - n * piece, 0), piece)
        if have:
            gg_ref[:, n * piece : n * piece + have] = rc[n, :, :have]
    for copy in sent:
        copy.wait_send()

    for c in range(chunks):
        depth = depth_of(c)
        host = chips - 1 - depth

        def drain(j, carry):
            @pl.when(z < host)
            def _():
                to_next(c, j).wait_send()

            to_mate(c, j).wait_send()
            return carry

        @pl.when(z <= host)
        def _():
            lax.fori_loop(0, z + 1, drain, 0)

        if depth:

            @pl.when(z == host)
            def _():
                for d in range(1, depth + 1):
                    to_mate(c, z + d).wait_send()
                    give_back(c, d).wait_send()

            @pl.when(z > host)
            def _():
                to_host(c).wait_send()
                query_to_host(c, 1).wait_send()


def shards(n_dp, n_seq, *args):
    tokens, base_query, k_base, v_base, cotangent, down, up, gate_weight = args
    rows, width = tokens.shape[1], base_query.shape[2]
    model, experts, total_rank = tokens.shape[2], gate_weight.shape[0], down.shape[1]
    head_count = width // HEAD_DIM
    heads = max(h for h in range(1, 5) if head_count % h == 0)
    chunks, chips = head_count // heads, n_seq // 2
    wide = heads * HEAD_DIM
    piece = -(-(model // 128) // n_seq) * 128
    any_spec = pl.BlockSpec(memory_space=pl.ANY)
    vmem_spec = pl.BlockSpec(memory_space=pltpu.VMEM)
    dma = pltpu.SemaphoreType.DMA
    return pl.pallas_call(
        functools.partial(kernel, chips, chunks, heads, n_dp),
        out_shape=(
            jax.ShapeDtypeStruct((1, rows, width), BF16),
            jax.ShapeDtypeStruct((experts, model), F32),
        ),
        in_specs=[any_spec] * 8,
        out_specs=(vmem_spec, vmem_spec),
        scratch_shapes=[
            pltpu.VMEM((chunks, chips, 2, 2, rows, wide), BF16),
            pltpu.VMEM((chunks, 3, 2, rows, wide), BF16),
            pltpu.VMEM((chunks, 3, rows, wide + total_rank), BF16),
            pltpu.VMEM((chunks, rows, wide + total_rank), BF16),
            pltpu.VMEM((heads, chips, rows, 2 * rows), F32),
            pltpu.VMEM((heads, rows, rows), F32),
            pltpu.VMEM((rows, width), BF16),
            pltpu.VMEM((rows, model), BF16),
            pltpu.VMEM((model, total_rank), BF16),
            pltpu.VMEM((total_rank, width), BF16),
            pltpu.VMEM((experts, model), BF16),
            pltpu.VMEM((rows, total_rank), BF16),
            pltpu.VMEM((rows, total_rank), F32),
            pltpu.VMEM((rows, experts), F32),
            pltpu.VMEM((n_seq, experts, piece), F32),
            pltpu.VMEM((n_seq, experts, piece), F32),
            pltpu.VMEM((n_dp, experts, piece), F32),
            pltpu.VMEM((n_seq, experts, piece), F32),
            dma((chunks, 2)),
            dma((5 + chunks,)),
            dma((chunks, chips)),
            dma((chunks, chips)),
            dma((chunks, chips)),
            dma((chunks, chips)),
            dma((chunks,)),
            dma((chunks, 3)),
            dma((chunks, 3)),
            dma((chunks,)),
            dma((n_seq,)),
            dma((n_seq,)),
            dma((n_dp,)),
            dma((n_dp,)),
            dma((n_seq,)),
            dma((n_seq,)),
        ],
        compiler_params=pltpu.CompilerParams(
            collective_id=0, has_side_effects=True, vmem_limit_bytes=56 * 1024 * 1024
        ),
        cost_estimate=pl.CostEstimate(
            flops=10 * rows * rows * n_seq * width, bytes_accessed=16 * rows * width,
            transcendentals=rows * rows * n_seq * head_count,
        ),
    )(k_base, v_base, base_query, cotangent, tokens, down, up, gate_weight)


def solution(mesh):
    split = P("dp", "seq", None)
    return jax.shard_map(
        functools.partial(shards, mesh.shape["dp"], mesh.shape["seq"]),
        mesh=mesh,
        in_specs=(split, split, split, split, split, P(), P(), P()),
        out_specs=(split, P()),
        check_vma=False,
    )
```

```python
import functools

import jax
import jax.numpy as jnp
from jax import lax
from jax.experimental import pallas as pl
from jax.experimental.pallas import tpu as pltpu
from jax.sharding import PartitionSpec as P

HEAD_DIM = 128
ADAPTER_SCALE = 2.0
MASKED = -1e30
MESH = pl.DeviceIdType.MESH
F32 = jnp.float32
BF16 = jnp.bfloat16
NT = (((1,), (1,)), ((), ()))
NN = (((1,), (0,)), ((), ()))


def dot(a, b, dims=NN, precision=None):
    return lax.dot_general(a, b, dims, preferred_element_type=F32, precision=precision)


def kernel(
    chips, chunks, heads, n_dp,
    k_hbm, v_hbm, bq_hbm, cot_hbm, tok_hbm, down_hbm, up_hbm, gw_hbm,
    out_ref, gg_ref,
    kv, qb, ob, back, sc, peak, bq, tok, down, up, gw, low, dmix, gates_ref, part, ra, rb, rc,
    own_sem, load_sem, up_send, up_recv, mate_send, mate_recv,
    q_send, q_recv, ret_send, ret_recv,
    a_send, a_recv, b_send, b_recv, c_send, c_recv,
):
    n_seq = 2 * chips
    me = lax.axis_index("seq")
    dp = lax.axis_index("dp")
    z = me // 2
    core = lax.rem(me, 2)
    mate = me + 1 - 2 * core
    rows = tok.shape[0]
    wide = heads * HEAD_DIM
    scale = HEAD_DIM ** (-0.5)

    barrier = pltpu.get_barrier_semaphore()
    for d in range(1, n_seq):
        pl.semaphore_signal(
            barrier, inc=1, device_id={"seq": lax.rem(me + d, n_seq)}, device_id_type=MESH
        )
    for d in range(1, n_dp):
        pl.semaphore_signal(
            barrier, inc=1, device_id={"dp": lax.rem(dp + d, n_dp)}, device_id_type=MESH
        )

    def depth_of(c):
        return min(max(0, 2 - c), chips - 1)

    def own_copies(c):
        cols = pl.ds(c * wide, wide)
        return [
            pltpu.make_async_copy(src.at[0, :, cols], kv.at[c, z, core, i], own_sem.at[c, i])
            for i, src in enumerate((k_hbm, v_hbm))
        ]

    for c in range(chunks):
        for copy in own_copies(c):
            copy.start()
    loads = [
        pltpu.make_async_copy(src, dst, load_sem.at[i])
        for i, (src, dst) in enumerate(
            (
                (tok_hbm.at[0], tok), (gw_hbm, gw), (down_hbm, down), (up_hbm, up),
                (bq_hbm.at[0], bq),
            )
        )
    ] + [
        pltpu.make_async_copy(
            cot_hbm.at[0, :, pl.ds(c * wide, wide)], qb.at[c, 0, 1], load_sem.at[5 + c]
        )
        for c in range(chunks)
    ]
    for copy in loads:
        copy.start()
    pl.semaphore_wait(barrier, n_seq - 1 + n_dp - 1)

    def block_copy(c, j, side, send, recv, target):
        block = kv.at[c, j, side]
        return pltpu.make_async_remote_copy(
            src_ref=block, dst_ref=block, send_sem=send.at[c, j], recv_sem=recv.at[c, j],
            device_id={"seq": target}, device_id_type=MESH,
        )

    def to_next(c, j):
        return block_copy(c, j, core, up_send, up_recv, lax.rem(me + 2, n_seq))

    def to_mate(c, j):
        return block_copy(c, j, core, mate_send, mate_recv, mate)

    def from_mate(c, j):
        return block_copy(c, j, 1 - core, mate_send, mate_recv, mate)

    def host_of(c):
        return 2 * (chips - 1 - depth_of(c)) + core

    def to_host(c):
        return block_copy(c, z, core, up_send, up_recv, host_of(c))

    def query_to_host(c, d):
        return pltpu.make_async_remote_copy(
            src_ref=qb.at[c, 0], dst_ref=qb.at[c, d], send_sem=q_send.at[c],
            recv_sem=q_recv.at[c, d], device_id={"seq": host_of(c)}, device_id_type=MESH,
        )

    def give_back(c, d):
        return pltpu.make_async_remote_copy(
            src_ref=ob.at[c, d], dst_ref=back.at[c], send_sem=ret_send.at[c, d],
            recv_sem=ret_recv.at[c], device_id={"seq": lax.rem(me + 2 * d, n_seq)},
            device_id_type=MESH,
        )

    for c in range(chunks):
        host = chips - 1 - depth_of(c)
        for copy in own_copies(c):
            copy.wait()

        @pl.when(z < host)
        def _():
            to_next(c, z).start()

        @pl.when(z <= host)
        def _():
            to_mate(c, z).start()

        @pl.when(z > host)
        def _():
            to_host(c).start()

    loads[0].wait()
    loads[1].wait()
    logits = dot(tok[...], gw[...], NT)
    logits = jnp.exp(logits - jnp.max(logits, axis=-1, keepdims=True))
    gates = logits / jnp.sum(logits, axis=-1, keepdims=True)
    gates_ref[...] = gates
    experts = gates.shape[1]
    total_rank = low.shape[1]
    rank = total_rank // experts
    spread = (
        lax.broadcasted_iota(jnp.int32, (experts, total_rank), 1) // rank
        == lax.broadcasted_iota(jnp.int32, (experts, total_rank), 0)
    ).astype(F32)
    loads[2].wait()
    low_b = dot(tok[...], down[...]).astype(BF16)
    low[...] = low_b
    wide_gates = dot(gates, spread, precision=lax.Precision.HIGHEST)
    mixed = (low_b.astype(F32) * wide_gates).astype(BF16)
    dmix[...] = jnp.zeros_like(dmix)
    for copy in loads[3:]:
        copy.wait()
    for c in range(chunks):
        cols = slice(c * wide, (c + 1) * wide)
        qb[c, 0, 0] = (
            bq[:, cols].astype(F32) + ADAPTER_SCALE * dot(mixed, up[:, cols])
        ).astype(BF16)
        for d in range(1, depth_of(c) + 1):

            @pl.when(z == chips - 1 - depth_of(c) + d)
            def _():
                query_to_host(c, d).start()

    def attend(c, d):
        cols = slice(c * wide, (c + 1) * wide)
        q_pos = core * rows + lax.broadcasted_iota(jnp.int32, (rows, 2 * rows), 0)
        visible = lax.broadcasted_iota(jnp.int32, (rows, 2 * rows), 1) <= q_pos
        heads_at = [slice(h * HEAD_DIM, (h + 1) * HEAD_DIM) for h in range(heads)]

        def fold(x, op):
            return op(x[:, :rows], x[:, rows:])

        last = z + d

        def score(j, h):
            keys = kv[c, j, :, 0, :, heads_at[h]].reshape(2 * rows, HEAD_DIM)
            return dot(qb[c, d, 0, :, heads_at[h]], keys, NT) * scale

        tops = []
        for h in range(heads):
            found = jnp.where(visible, score(last, h), MASKED)
            sc[h, last] = found
            tops.append(fold(found, jnp.maximum))

        def first_pass(j, tops):
            new_tops = []
            for h in range(heads):
                found = score(j, h)
                sc[h, j] = found
                new_tops.append(jnp.maximum(tops[h], fold(found, jnp.maximum)))
            return tuple(new_tops)

        tops = lax.fori_loop(0, last, first_pass, tuple(tops))
        for h in range(heads):
            peak[h] = jnp.broadcast_to(
                jnp.max(tops[h], axis=-1, keepdims=True), (rows, rows)
            )

        def second_pass(j, states):
            new_states = []
            for h in range(heads):
                total, delta, vk, grad = states[h]
                keys = kv[c, j, :, 0, :, heads_at[h]].reshape(2 * rows, HEAD_DIM)
                values = kv[c, j, :, 1, :, heads_at[h]].reshape(2 * rows, HEAD_DIM)
                slopes = dot(qb[c, d, 1, :, heads_at[h]], values, NT)
                top = peak[h]
                weights = jnp.exp(sc[h, j] - jnp.concatenate([top, top], axis=1))
                products = weights * slopes
                new_states.append(
                    (
                        total + fold(weights, jnp.add),
                        delta + fold(products, jnp.add),
                        vk + dot(weights.astype(BF16), jnp.concatenate([values, keys], axis=1)),
                        grad + dot(products.astype(BF16), keys),
                    )
                )
            return tuple(new_states)

        empty = jnp.zeros((rows, rows), F32)
        zero = jnp.zeros((rows, HEAD_DIM), F32)
        zeros = jnp.zeros((rows, 2 * HEAD_DIM), F32)
        states = lax.fori_loop(
            0, last + 1, second_pass, ((empty, empty, zeros, zero),) * heads
        )
        outs = []
        grads = []
        for total, delta, vk, grad in states:
            inverse = 1.0 / jnp.sum(total, axis=-1, keepdims=True)
            delta = jnp.sum(delta, axis=-1, keepdims=True)
            outs.append((vk[:, :HEAD_DIM] * inverse).astype(BF16))
            grads.append(
                (
                    scale
                    * (
                        grad * inverse
                        - (delta * inverse) * (vk[:, HEAD_DIM:] * inverse)
                    )
                ).astype(BF16)
            )
        return (
            jnp.concatenate(outs, axis=1),
            dot(jnp.concatenate(grads, axis=1), up[:, cols], NT),
        )

    def own_step(c):
        host = chips - 1 - depth_of(c)
        for gap in range(1, host + 1):

            @pl.when((z >= gap) & (z <= host))
            def _():
                to_next(c, z - gap).wait_recv()

                @pl.when(z < host)
                def _():
                    to_next(c, z - gap).start()

                to_mate(c, z - gap).start()

        @pl.when(z <= host)
        def _():
            def arrive(gap, carry):
                from_mate(c, z - gap).wait_recv()
                return carry

            lax.fori_loop(0, z + 1, arrive, 0)
            attended, term = attend(c, 0)
            out_ref[0, :, c * wide : (c + 1) * wide] = attended
            dmix[...] += term

    def hosted_step(c):
        host = chips - 1 - depth_of(c)

        @pl.when(z == host)
        def _():
            for d in range(1, depth_of(c) + 1):
                to_next(c, z + d).wait_recv()
                to_mate(c, z + d).start()
            for d in range(1, depth_of(c) + 1):
                from_mate(c, z + d).wait_recv()
                query_to_host(c, d).wait_recv()
                attended, term = attend(c, d)
                ob[c, d, :, :wide] = attended
                ob[c, d, :, wide:] = term.astype(BF16)
                give_back(c, d).start()

    deep = [c for c in range(chunks) if depth_of(c) > 1]
    waiting = []
    for c in range(chunks):
        own_step(c)
        if c == chunks - 1:
            waiting += deep
        for late in waiting:
            hosted_step(late)
        waiting = [c] if depth_of(c) == 1 else []
    for late in waiting:
        hosted_step(late)

    for c in range(chunks):
        if depth_of(c):

            @pl.when(z > chips - 1 - depth_of(c))
            def _():
                give_back(c, 1).wait_recv()
                out_ref[0, :, c * wide : (c + 1) * wide] = back[c, :, :wide]
                dmix[...] += back[c, :, wide:].astype(F32)

    dgates = dot(
        ADAPTER_SCALE * dmix[...] * low[...].astype(F32), spread, NT,
        precision=lax.Precision.HIGHEST,
    )
    gates = gates_ref[...]
    dlogits = gates * (dgates - jnp.sum(gates * dgates, axis=-1, keepdims=True))
    partial = dot(dlogits.astype(BF16), tok[...], (((0,), (0,)), ((), ())))

    piece = part.shape[2]
    full = partial.shape[1]
    for n in range(n_seq):
        have = min(max(full - n * piece, 0), piece)
        if have:
            part[n, :, :have] = partial[:, n * piece : n * piece + have]
        if have < piece:
            part[n, :, have:] = jnp.zeros((part.shape[1], piece - have), F32)

    def exchange(axis, index, count, source, target, send, recv):
        copies = []
        for d in range(1, count):
            peer = lax.rem(index + d, count)
            copies.append(
                pltpu.make_async_remote_copy(
                    src_ref=source(peer), dst_ref=target.at[index],
                    send_sem=send.at[d], recv_sem=recv.at[index],
                    device_id={axis: peer}, device_id_type=MESH,
                )
            )
        for copy in copies:
            copy.start()
        for d in range(1, count):
            peer = lax.rem(index + d, count)
            pltpu.make_async_remote_copy(
                src_ref=source(peer), dst_ref=target.at[peer],
                send_sem=send.at[d], recv_sem=recv.at[peer],
                device_id={axis: peer}, device_id_type=MESH,
            ).wait_recv()
        return copies

    ra[me] = part[me]
    sent = exchange("seq", me, n_seq, lambda peer: part.at[peer], ra, a_send, a_recv)
    total = ra[0]
    for n in range(1, n_seq):
        total = total + ra[n]
    rb[dp] = total
    sent += exchange("dp", dp, n_dp, lambda peer: rb.at[dp], rb, b_send, b_recv)
    total = rb[0]
    for n in range(1, n_dp):
        total = total + rb[n]
    rc[me] = total
    sent += exchange("seq", me, n_seq, lambda peer: rc.at[me], rc, c_send, c_recv)
    for n in range(n_seq):
        have = min(max(full - n * piece, 0), piece)
        if have:
            gg_ref[:, n * piece : n * piece + have] = rc[n, :, :have]
    for copy in sent:
        copy.wait_send()

    for c in range(chunks):
        depth = depth_of(c)
        host = chips - 1 - depth

        def drain(j, carry):
            @pl.when(z < host)
            def _():
                to_next(c, j).wait_send()

            to_mate(c, j).wait_send()
            return carry

        @pl.when(z <= host)
        def _():
            lax.fori_loop(0, z + 1, drain, 0)

        if depth:

            @pl.when(z == host)
            def _():
                for d in range(1, depth + 1):
                    to_mate(c, z + d).wait_send()
                    give_back(c, d).wait_send()

            @pl.when(z > host)
            def _():
                to_host(c).wait_send()
                query_to_host(c, 1).wait_send()


def shards(n_dp, n_seq, *args):
    tokens, base_query, k_base, v_base, cotangent, down, up, gate_weight = args
    rows, width = tokens.shape[1], base_query.shape[2]
    model, experts, total_rank = tokens.shape[2], gate_weight.shape[0], down.shape[1]
    head_count = width // HEAD_DIM
    heads = max(h for h in range(1, 5) if head_count % h == 0)
    chunks, chips = head_count // heads, n_seq // 2
    wide = heads * HEAD_DIM
    piece = -(-(model // 128) // n_seq) * 128
    any_spec = pl.BlockSpec(memory_space=pl.ANY)
    vmem_spec = pl.BlockSpec(memory_space=pltpu.VMEM)
    dma = pltpu.SemaphoreType.DMA
    return pl.pallas_call(
        functools.partial(kernel, chips, chunks, heads, n_dp),
        out_shape=(
            jax.ShapeDtypeStruct((1, rows, width), BF16),
            jax.ShapeDtypeStruct((experts, model), F32),
        ),
        in_specs=[any_spec] * 8,
        out_specs=(vmem_spec, vmem_spec),
        scratch_shapes=[
            pltpu.VMEM((chunks, chips, 2, 2, rows, wide), BF16),
            pltpu.VMEM((chunks, 3, 2, rows, wide), BF16),
            pltpu.VMEM((chunks, 3, rows, wide + total_rank), BF16),
            pltpu.VMEM((chunks, rows, wide + total_rank), BF16),
            pltpu.VMEM((heads, chips, rows, 2 * rows), F32),
            pltpu.VMEM((heads, rows, rows), F32),
            pltpu.VMEM((rows, width), BF16),
            pltpu.VMEM((rows, model), BF16),
            pltpu.VMEM((model, total_rank), BF16),
            pltpu.VMEM((total_rank, width), BF16),
            pltpu.VMEM((experts, model), BF16),
            pltpu.VMEM((rows, total_rank), BF16),
            pltpu.VMEM((rows, total_rank), F32),
            pltpu.VMEM((rows, experts), F32),
            pltpu.VMEM((n_seq, experts, piece), F32),
            pltpu.VMEM((n_seq, experts, piece), F32),
            pltpu.VMEM((n_dp, experts, piece), F32),
            pltpu.VMEM((n_seq, experts, piece), F32),
            dma((chunks, 2)),
            dma((5 + chunks,)),
            dma((chunks, chips)),
            dma((chunks, chips)),
            dma((chunks, chips)),
            dma((chunks, chips)),
            dma((chunks,)),
            dma((chunks, 3)),
            dma((chunks, 3)),
            dma((chunks,)),
            dma((n_seq,)),
            dma((n_seq,)),
            dma((n_dp,)),
            dma((n_dp,)),
            dma((n_seq,)),
            dma((n_seq,)),
        ],
        compiler_params=pltpu.CompilerParams(
            collective_id=0, has_side_effects=True, vmem_limit_bytes=56 * 1024 * 1024
        ),
        cost_estimate=pl.CostEstimate(
            flops=10 * rows * rows * n_seq * width, bytes_accessed=16 * rows * width,
            transcendentals=rows * rows * n_seq * head_count,
        ),
    )(k_base, v_base, base_query, cotangent, tokens, down, up, gate_weight)


def solution(mesh):
    split = P("dp", "seq", None)
    return jax.shard_map(
        functools.partial(shards, mesh.shape["dp"], mesh.shape["seq"]),
        mesh=mesh,
        in_specs=(split, split, split, split, split, P(), P(), P()),
        out_specs=(split, P()),
        check_vma=False,
    )
```
